32 devices in a mesh: blk: 8 (over z, x), quarter: 4 (over y, core).
Axes of the slice: x: 2, y: 2, z: 4, core: 2. Of those that a mesh axis runs over, the one named last changes fastest.
Arguments:
- bints: bfloat16 [64, 512, 1280], P('blk', None, 'quarter'), may hold values from -2.5 to 2.5
- occ_energy: float32 [64], replicated, may hold values from -2 to -0.5
- vir_energy: float32 [512], replicated, may hold values from 0.2 to 3
Outputs:
- gamma: float32 [64, 512, 1280], P(('blk', 'quarter'))
- vvdens: float32 [512, 512], P(('blk', 'quarter'))
The draws below stay inside these ranges and needn't reach their ends.
All inputs are finite; a program needn't handle non-finite values.
Results may differ from the reference program's by a relative error of at most 0.0016.
Values may be sent and summed in bfloat16 or wider, within the bound.
No kernel may reach another device: no remote copies, remote signals or barrier semaphores. Data moves between devices by JAX's collectives and lax.ppermute only.
A program may use at most 128 MiB of HBM per device.

```python
import jax
import jax.numpy as jnp
from jax import lax

V = 512
NAUX = 1280
OCC_DEV = 2
CYCLE = 3
O = 64
PAIRS = 384
N_BLK = 8
N_QUARTER = 4


def shard_levels(own_key, extent, pieces, least, high):
    gain = 1.0
    for dim, parts in pieces:
        heights = jax.random.uniform(jax.random.fold_in(jax.random.fold_in(own_key, 6), dim), (parts,), jnp.float32, least / len(pieces), high / len(pieces))
        gain = gain * jnp.repeat(jnp.exp(heights), extent[dim] // parts).reshape((-1,) + (1,) * (len(extent) - 1 - dim))
    return gain


def noise(rng, shape, width, most, split=(), kind=jnp.bfloat16):
    array = width * jax.random.normal(rng, shape, jnp.float32)
    if split:
        array = array * shard_levels(rng, shape, split, -0.22, 0.18)
    return jnp.clip(array, -most, most).astype(kind)


def setup_inputs(seed: int = 0) -> dict:
    splits = jax.random.split(jax.random.key(seed), 4)
    return {
        "bints": noise(splits[0], (O, V, NAUX), (NAUX ** -0.25), 2.5, ((0, 8), (2, 4))),
        "occ_energy": jnp.clip(jax.random.uniform(splits[1], (O,), jnp.float32, -2.0, -0.5), -2.0, -0.5),
        "vir_energy": jnp.clip(jax.random.uniform(splits[2], (V,), jnp.float32, 0.2, 3.0), 0.2, 3.0),
    }


def reference(bints, occ_energy, vir_energy):
    groups = O // OCC_DEV
    blocks = bints.reshape(groups, OCC_DEV, V, NAUX)
    energies = occ_energy.reshape(groups, OCC_DEV)

    def per_group(carry, group):
        block_id = group // N_QUARTER
        quarter_id = group % N_QUARTER
        own = blocks[group].astype(jnp.float32)
        own_energy = energies[group]
        density = jnp.zeros((OCC_DEV, V, NAUX), jnp.float32)
        for step in range(CYCLE):
            partner = (((block_id - step) % N_BLK) * N_QUARTER + quarter_id).astype(jnp.int32)
            other = blocks[partner].astype(jnp.float32)
            other_energy = energies[partner]
            pairint = jnp.einsum("iap,jbp->ijab", own, other)
            denom = (vir_energy[None, None, :, None] + vir_energy[None, None, None, :]
                     - own_energy[:, None, None, None] - other_energy[None, :, None, None])
            amp = pairint / denom
            amp_b = amp.astype(jnp.bfloat16).astype(jnp.float32)
            tilde = (2.0 * amp - jnp.swapaxes(amp, 2, 3)).astype(jnp.bfloat16).astype(jnp.float32)
            density = density + jnp.einsum("ijab,jbp->iap", tilde, other)
            carry = carry + jnp.einsum("ijac,ijbc->ab", amp_b, tilde)
        return carry, density

    total, gammas = lax.scan(per_group, jnp.zeros((V, V), jnp.float32), jnp.arange(groups, dtype=jnp.int32))
    return gammas.reshape(O, V, NAUX), total / PAIRS
```

```python
import jax
import jax.numpy as jnp
from jax import lax
from jax.experimental import pallas as pl
from jax.experimental.pallas import tpu as pltpu
from jax.sharding import PartitionSpec as P

CYCLE = 3
CHUNKS = ((0, 0, 256), (0, 256, 256), (1, 0, 256), (1, 256, 128), (1, 384, 128))
TILE = 256
F32, BF16 = jnp.float32, jnp.bfloat16
NT = (((1,), (1,)), ((), ()))


def whole(space=None):
    return pl.BlockSpec(memory_space=pltpu.VMEM if space is None else space)


def call(body, out_shape, in_specs, out_specs, scratch=(), aliases=None, flops=0, limit=8):
    return pl.pallas_call(
        body,
        out_shape=out_shape,
        in_specs=in_specs,
        out_specs=out_specs,
        scratch_shapes=list(scratch),
        input_output_aliases=aliases or {},
        compiler_params=pltpu.CompilerParams(vmem_limit_bytes=limit * 1024 * 1024),
        cost_estimate=pl.CostEstimate(flops=flops, bytes_accessed=0, transcendentals=0),
    )


def slices(bints, quarter_id, groups, quarters):
    depth = bints.shape[1]
    jobs = []
    for chunks in groups:
        for d in range(quarters):
            at = 0
            for k in chunks:
                jobs.append((len(jobs), k, d, at))
                at += CHUNKS[k][2]
    widths = [sum(CHUNKS[k][2] for k in chunks) for chunks in groups]

    def body(q_ref, src, *rest):
        outs, sems = rest[:-1], rest[-1]
        copies = []
        for g, chunks in enumerate(groups):
            for d in range(quarters):
                target = lax.rem(q_ref[0] + d, quarters)
                at = 0
                for k in chunks:
                    orb, first, rows = CHUNKS[k]
                    copies.append(
                        pltpu.make_async_copy(
                            src.at[2 * target + orb, :, pl.ds(first, rows)],
                            outs[g * quarters + d].at[:, pl.ds(at, rows)],
                            sems.at[len(copies)],
                        )
                    )
                    copies[-1].start()
                    at += rows
        for copy in copies:
            copy.wait()

    shapes = [jax.ShapeDtypeStruct((depth, w), BF16) for w in widths for _ in range(quarters)]
    flat = call(
        body,
        shapes,
        [whole(pltpu.SMEM), whole(pltpu.HBM)],
        [whole()] * len(shapes),
        [pltpu.SemaphoreType.DMA((len(jobs),))],
    )(quarter_id, bints)
    return [flat[g * quarters : (g + 1) * quarters] for g in range(len(groups))]


def joined(pieces, quarter_id, chunks):
    quarters = len(pieces)
    depth = pieces[0].shape[0]

    def body(q_ref, *refs):
        ins, outs = refs[:quarters], refs[quarters:]
        for d in range(quarters):
            source = lax.rem(q_ref[0] + quarters - d, quarters)
            rows = pl.ds(pl.multiple_of(source * depth, 64), depth)
            at = 0
            for out, k in zip(outs, chunks):
                out[rows, :] = ins[d][:, at : at + CHUNKS[k][2]]
                at += CHUNKS[k][2]

    return call(
        body,
        [jax.ShapeDtypeStruct((quarters * depth, CHUNKS[k][2]), BF16) for k in chunks],
        [whole(pltpu.SMEM)] + [whole()] * quarters,
        [whole()] * len(chunks),
    )(quarter_id, *pieces)


def tiles_of(refs, orb):
    found = []
    for ref, (o, first, rows) in zip(refs, CHUNKS):
        if o != orb:
            continue
        if found and found[-1][1] + rows <= TILE:
            found[-1] = (found[-1][0], found[-1][1] + rows, found[-1][2] + [ref])
        else:
            found.append((first, rows, [ref]))
    return found


def side_by_side(values):
    return values[0] if len(values) == 1 else jnp.concatenate(values, axis=1)


def amplitudes(left, tiles, col, row, e_left, e_right, amp):
    for first, width, refs in tiles:
        right = side_by_side([ref[...] for ref in refs])
        pairint = jnp.dot(left[...], right, preferred_element_type=F32)
        denom = col[...] + row[:, first : first + width] - e_left - e_right
        amp[:, first : first + width] = pairint / denom


def finish_pair(amp, amp_b, tilde, vv):
    size = amp.shape[0]
    for fa in range(0, size, TILE):
        for fb in range(0, size, TILE):
            here = amp[fa : fa + TILE, fb : fb + TILE]
            there = amp[fb : fb + TILE, fa : fa + TILE]
            amp_b[fa : fa + TILE, fb : fb + TILE] = here.astype(BF16)
            tilde[fa : fa + TILE, fb : fb + TILE] = (2.0 * here - there.T).astype(BF16)
    vv[...] += lax.dot_general(amp_b[...], tilde[...], NT, preferred_element_type=F32)


def pair_flops(n, naux, count):
    return count * (2 * n * n * naux + 2 * n * n * n)


def own_pairs(own, energies, col, row):
    n, naux = col.shape[0], own[0].shape[0]

    def body(e_ref, col_ref, row_ref, *refs):
        own_refs = refs[: len(CHUNKS)]
        nat, t0, t1, vv, amp, amp_b = refs[len(CHUNKS) :]
        vv[...] = jnp.zeros_like(vv)
        for ref, (orb, first, rows) in zip(own_refs, CHUNKS):
            nat[orb, first : first + rows, :] = ref[...].T
        for j, tilde in enumerate((t0, t1)):
            for i in range(2):
                amplitudes(nat.at[i], tiles_of(own_refs, j), col_ref, row_ref, e_ref[i], e_ref[2 + j], amp)
                finish_pair(amp, amp_b, tilde.at[i], vv)

    shapes = [jax.ShapeDtypeStruct((2, n, naux), BF16)]
    shapes += [jax.ShapeDtypeStruct((2, n, n), BF16)] * 2
    shapes += [jax.ShapeDtypeStruct((n, n), F32)]
    return call(
        body, shapes, [whole(pltpu.SMEM)] + [whole()] * (2 + len(CHUNKS)), [whole()] * 4,
        [pltpu.VMEM((n, n), F32), pltpu.VMEM((n, n), BF16)], flops=pair_flops(n, naux, 4),
    )(energies, col, row, *own)


def other_pairs(nat, others, orb, energies, col, row, vv):
    n, naux = col.shape[0], nat.shape[2]
    used = [k for k, (o, _, _) in enumerate(CHUNKS) if o == orb]

    def body(e_ref, col_ref, row_ref, nat_ref, *refs):
        other_refs = [None] * len(CHUNKS)
        for k, ref in zip(used, refs):
            other_refs[k] = ref
        vv_in, tilde, vv, amp, amp_b = refs[len(used) :]
        vv[...] = vv_in[...]
        for i in range(2):
            amplitudes(nat_ref.at[i], tiles_of(other_refs, orb), col_ref, row_ref, e_ref[i], e_ref[2 + orb], amp)
            finish_pair(amp, amp_b, tilde.at[i], vv)

    return call(
        body,
        [jax.ShapeDtypeStruct((2, n, n), BF16), jax.ShapeDtypeStruct((n, n), F32)],
        [whole(pltpu.SMEM)] + [whole()] * (4 + len(used)),
        [whole()] * 2,
        [pltpu.VMEM((n, n), F32), pltpu.VMEM((n, n), BF16)],
        flops=pair_flops(n, naux, 2),
    )(energies, col, row, nat, *(others[k] for k in used), vv)


def gamma(which, tildes, groups, before=None):
    n, naux = tildes[0].shape[1], groups[0][0].shape[0]
    steps = naux // TILE

    def body(*refs):
        refs = list(refs)
        if before is not None:
            refs.pop(0)
        t_refs = [refs.pop(0) for _ in tildes]
        g_refs = [[refs.pop(0) for _ in CHUNKS] for _ in groups]
        out, buf, sems = refs

        def copy(p):
            return pltpu.make_async_copy(
                buf.at[p % 2], out.at[which, :, pl.ds(p * TILE, TILE)], sems.at[p % 2]
            )

        for p in range(steps):
            if p >= 2:
                copy(p - 2).wait()
            total = None
            for g in range(len(groups)):
                for orb in range(2):
                    right = side_by_side(
                        [
                            ref[p * TILE : (p + 1) * TILE, :]
                            for ref, (o, _, _) in zip(g_refs[g], CHUNKS)
                            if o == orb
                        ]
                    )
                    part = lax.dot_general(t_refs[2 * g + orb][which], right, NT, preferred_element_type=F32)
                    total = part if total is None else total + part
            buf[p % 2] = total
            copy(p).start()
        for p in range(max(steps - 2, 0), steps):
            copy(p).wait()

    arrays = [*tildes, *(c for g in groups for c in g)]
    specs = [whole()] * len(arrays)
    aliases = None
    if before is not None:
        arrays.insert(0, before)
        specs.insert(0, whole(pltpu.HBM))
        aliases = {0: 0}
    return call(
        body,
        jax.ShapeDtypeStruct((2, n, naux), F32),
        specs,
        whole(pltpu.HBM),
        [pltpu.VMEM((2, n, TILE), F32), pltpu.SemaphoreType.DMA((2,))],
        aliases,
        flops=2 * n * n * naux * len(tildes),
    )(*arrays)


def split_by_quarter(vv, quarter_id, quarters, blocks):
    n = vv.shape[0]
    rows = vv.reshape(blocks, quarters, n // (quarters * blocks), n)
    pick = lambda d: lax.dynamic_index_in_dim(rows, (quarter_id + d) % quarters, 1, keepdims=False)
    return [pick(0)] + [pick(d).astype(BF16) for d in range(1, quarters)]


def per_device(bints, occ_energy, vir_energy):
    quarters = lax.axis_size("quarter")
    blocks = lax.axis_size("blk")
    block_id = lax.axis_index("blk")
    quarter_id = lax.axis_index("quarter")
    odd = lax.rem(block_id, 2) == 1
    n = bints.shape[1]
    q = jnp.reshape(quarter_id, (1,)).astype(jnp.int32)

    def energies(step):
        group = (block_id + blocks - step) % blocks * quarters + quarter_id
        return lax.dynamic_slice_in_dim(occ_energy, group * 2, 2)

    def on_blk(x, by):
        return lax.ppermute(x, "blk", [(i, (i + by) % blocks) for i in range(blocks)])

    def swapped(x):
        return lax.ppermute(x, "blk", [(i, i ^ 1) for i in range(blocks)])

    def on_quarter(x, by):
        return lax.ppermute(x, "quarter", [(i, (i + by) % quarters) for i in range(quarters)])

    def on_both(x, by):
        return lax.ppermute(
            x,
            ("blk", "quarter"),
            [
                (b * quarters + k, (b + 2) % blocks * quarters + (k + by) % quarters)
                for b in range(blocks)
                for k in range(quarters)
            ],
        )

    by_aux = jnp.swapaxes(bints, 1, 2)
    piece1, piece0 = slices(by_aux, q, ((1,), (0,)), quarters)
    (rest,) = slices(by_aux, q, ((0, 2, 3, 4),), quarters)

    own, two = [None] * 5, [None] * 5
    (own[1],) = joined([piece1[0]] + [on_quarter(piece1[d], d) for d in range(1, quarters)], q, (1,))
    (two[0],) = joined([on_both(piece0[d], d) for d in range(quarters)], q, (0,))
    two[1] = on_blk(own[1], 2)
    own[0], own[2], own[3], own[4] = joined(
        [rest[0]] + [on_quarter(rest[d], d) for d in range(1, quarters)], q, (0, 2, 3, 4)
    )
    for k in (2, 3, 4):
        two[k] = on_blk(own[k], 2)
    one = [None] * 5
    first = swapped(jnp.where(odd, two[0], own[1]))
    second = swapped(jnp.where(odd, two[1], own[0]))
    one[0] = jnp.where(odd, second, first)
    one[1] = jnp.where(odd, first, second)
    for k in (2, 3, 4):
        one[k] = swapped(jnp.where(odd, two[k], own[k]))

    col, row = vir_energy[:, None], vir_energy[None, :]
    mine = energies(0)
    e0 = jnp.concatenate([mine, mine])
    e1 = jnp.concatenate([mine, energies(1)])
    e2 = jnp.concatenate([mine, energies(2)])
    nat, t00, t01, vv = own_pairs(own, e0, col, row)
    t20, vv = other_pairs(nat, two, 0, e2, col, row, vv)
    t10, vv = other_pairs(nat, one, 0, e1, col, row, vv)
    t21, vv = other_pairs(nat, two, 1, e2, col, row, vv)
    t11, vv = other_pairs(nat, one, 1, e1, col, row, vv)

    kept, *sent = split_by_quarter(vv, quarter_id, quarters, blocks)
    came = [on_quarter(s, d + 1) for d, s in enumerate(sent)]
    tildes = [t00, t01, t10, t11, t20, t21]
    groups = [own, one, two]
    density = gamma(0, tildes, groups)
    density, came = lax.optimization_barrier((density, came))
    total = kept + sum(c.astype(F32) for c in came)
    density = gamma(1, tildes, groups, density)

    part = n // (quarters * blocks)
    bit = 1
    while bit < blocks:
        mask = bit
        total = total.reshape(-1, 2, part, n)
        up = lax.rem(block_id // bit, 2)
        keep = lax.dynamic_index_in_dim(total, up, 1, keepdims=False)
        give = lax.dynamic_index_in_dim(total, 1 - up, 1, keepdims=False)
        got = lax.ppermute(give, "blk", [(i, i ^ mask) for i in range(blocks)])
        if bit == 1:
            density, got = lax.optimization_barrier((density, got))
        total = keep + got
        bit *= 2
    window = 2 * quarters * blocks * CYCLE * 2
    return density, total.reshape(part, n) / float(window)


def solution(mesh):
    return jax.shard_map(
        per_device,
        mesh=mesh,
        in_specs=(P("blk", None, "quarter"), P(), P()),
        out_specs=(P(("blk", "quarter"), None, None), P(("blk", "quarter"), None)),
        check_vma=False,
    )
```

```python
import jax
import jax.numpy as jnp
from jax import lax
from jax.experimental import pallas as pl
from jax.experimental.pallas import tpu as pltpu
from jax.sharding import PartitionSpec as P

CYCLE = 3
TILE = 256
F32, BF16 = jnp.float32, jnp.bfloat16
NT = (((1,), (1,)), ((), ()))


def whole(space=None):
    return pl.BlockSpec(memory_space=pltpu.VMEM if space is None else space)


def call(body, out_shape, in_specs, out_specs, scratch=(), aliases=None, flops=0, limit=8):
    return pl.pallas_call(
        body,
        out_shape=out_shape,
        in_specs=in_specs,
        out_specs=out_specs,
        scratch_shapes=list(scratch),
        input_output_aliases=aliases or {},
        compiler_params=pltpu.CompilerParams(vmem_limit_bytes=limit * 1024 * 1024),
        cost_estimate=pl.CostEstimate(flops=flops, bytes_accessed=0, transcendentals=0),
    )


def slices(bints, quarter_id, raw, groups, quarters):
    depth = bints.shape[1]

    def body(q_ref, src, *rest):
        outs, sems = rest[:-1], rest[-1]
        copies = []

        def copy(span, e, dst):
            orb, first, rows = span
            where = src.at[2 * (q_ref[0] ^ e) + orb, :, pl.ds(first, rows)]
            copies.append(pltpu.make_async_copy(where, dst, sems.at[len(copies)]))
            copies[-1].start()

        for g, span in enumerate(groups):
            for e in range(quarters):
                copy(span, e, outs[1 + g * quarters + e])
        for e in range(quarters):
            copy(raw, e, outs[0].at[e])
        for c in copies:
            c.wait()

    shapes = [jax.ShapeDtypeStruct((quarters, depth, raw[2]), BF16)]
    shapes += [jax.ShapeDtypeStruct((depth, span[2]), BF16) for span in groups for _ in range(quarters)]
    flat = call(
        body,
        shapes,
        [whole(pltpu.SMEM), whole(pltpu.HBM)],
        [whole()] * len(shapes),
        [pltpu.SemaphoreType.DMA((quarters * (1 + len(groups)),))],
    )(quarter_id, bints)
    return flat[0], [flat[1 + g * quarters : 1 + (g + 1) * quarters] for g in range(len(groups))]


def joined(pieces, quarter_id, widths):
    depth = pieces[0].shape[0]

    def body(q_ref, *refs):
        ins, outs = refs[: len(pieces)], refs[len(pieces) :]
        for e, ref in enumerate(ins):
            rows = pl.ds(pl.multiple_of((q_ref[0] ^ e) * depth, 64), depth)
            at = 0
            for out, width in zip(outs, widths):
                out[rows, :] = ref[:, at : at + width]
                at += width

    return call(
        body,
        [jax.ShapeDtypeStruct((len(pieces) * depth, width), BF16) for width in widths],
        [whole(pltpu.SMEM)] + [whole()] * len(pieces),
        [whole()] * len(widths),
    )(quarter_id, *pieces)


def tiles_of(refs, first=0):
    found = []
    for ref in refs:
        for at in range(0, ref.shape[1], TILE):
            view = ref.at[:, at : min(at + TILE, ref.shape[1])]
            width = view.shape[1]
            if found and found[-1][1] + width <= TILE:
                found[-1] = (found[-1][0], found[-1][1] + width, found[-1][2] + [view])
            else:
                found.append((first, width, [view]))
            first += width
    return found


def side_by_side(values):
    return values[0] if len(values) == 1 else jnp.concatenate(values, axis=1)


def amplitudes(left, parts, first, col, row, e_left, e_right, amp):
    for at, width, views in tiles_of(parts, first):
        right = side_by_side([view[...] for view in views])
        pairint = jnp.dot(left[...], right, preferred_element_type=F32)
        cols = slice(at, at + width)
        amp[:, cols] = pairint / (col[...] + row[:, cols] - e_left - e_right)


def finish_pair(amp, amp_b, tilde, vv):
    size = amp.shape[0]
    for fa in range(0, size, TILE):
        for fb in range(0, size, TILE):
            here = amp[fa : fa + TILE, fb : fb + TILE]
            there = amp[fb : fb + TILE, fa : fa + TILE]
            amp_b[fa : fa + TILE, fb : fb + TILE] = here.astype(BF16)
            tilde[fa : fa + TILE, fb : fb + TILE] = (2.0 * here - there.T).astype(BF16)
    vv[...] += lax.dot_general(amp_b[...], tilde[...], NT, preferred_element_type=F32)


def pair_flops(n, naux, count):
    return count * 2 * n * n * (naux + n)


def own_pairs(own, energies, col, row):
    n = col.shape[0]
    naux = own[0][0].shape[0]
    counts = [len(parts) for parts in own]

    def body(e_ref, col_ref, row_ref, *refs):
        parts = [refs[: counts[0]], refs[counts[0] : sum(counts)]]
        nat, t0, t1, vv, amp, amp_b = refs[sum(counts) :]
        vv[...] = jnp.zeros_like(vv)
        for j in range(2):
            for first, width, views in tiles_of(parts[j]):
                nat[j, first : first + width, :] = side_by_side([view[...] for view in views]).T
        for j, tilde in enumerate((t0, t1)):
            for i in range(2):
                amplitudes(nat.at[i], parts[j], 0, col_ref, row_ref, e_ref[i], e_ref[2 + j], amp)
                finish_pair(amp, amp_b, tilde.at[i], vv)

    return call(
        body,
        [
            jax.ShapeDtypeStruct((2, n, naux), BF16),
            jax.ShapeDtypeStruct((2, n, n), BF16),
            jax.ShapeDtypeStruct((2, n, n), BF16),
            jax.ShapeDtypeStruct((n, n), F32),
        ],
        [whole(pltpu.SMEM)] + [whole()] * (2 + sum(counts)),
        [whole()] * 4,
        [pltpu.VMEM((n, n), F32), pltpu.VMEM((n, n), BF16)],
        flops=pair_flops(n, naux, 4),
    )(energies, col, row, *own[0], *own[1])


def other_pairs(nat, parts, orb, energies, col, row, vv):
    n = col.shape[0]

    def body(e_ref, col_ref, row_ref, nat_ref, *refs):
        part_refs = refs[: len(parts)]
        vv_in, tilde, vv, amp, amp_b = refs[len(parts) :]
        vv[...] = vv_in[...]
        for i in range(2):
            amplitudes(nat_ref.at[i], part_refs, 0, col_ref, row_ref, e_ref[i], e_ref[2 + orb], amp)
            finish_pair(amp, amp_b, tilde.at[i], vv)

    return call(
        body,
        [jax.ShapeDtypeStruct((2, n, n), BF16), jax.ShapeDtypeStruct(vv.shape, F32)],
        [whole(pltpu.SMEM)] + [whole()] * (4 + len(parts)),
        [whole()] * 2,
        [pltpu.VMEM((n, n), F32), pltpu.VMEM((n, n), BF16)],
        flops=pair_flops(n, nat.shape[2], 2),
    )(energies, col, row, nat, *parts, vv)


def first_columns(nat, parts, orb, energies, col, row):
    n = col.shape[0]
    wide = sum(part.shape[1] for part in parts)

    def body(e_ref, col_ref, row_ref, nat_ref, *refs):
        for i in range(2):
            amplitudes(nat_ref.at[i], refs[:-1], 0, col_ref, row_ref, e_ref[i], e_ref[2 + orb], refs[-1].at[i])

    return call(
        body,
        jax.ShapeDtypeStruct((2, n, wide), F32),
        [whole(pltpu.SMEM)] + [whole()] * (3 + len(parts)),
        whole(),
        flops=2 * 2 * n * wide * nat.shape[2],
    )(energies, col, row, nat, *parts)


def last_columns(nat, parts, orb, energies, col, row, amps, vv):
    n = col.shape[0]
    known = amps.shape[2]

    def body(e_ref, col_ref, row_ref, nat_ref, *refs):
        part_refs = refs[: len(parts)]
        amp_in, vv_in, tilde, vv, amp, amp_b = refs[len(parts) :]
        vv[...] = vv_in[...]
        for i in range(2):
            amp[:, :known] = amp_in[i]
            amplitudes(nat_ref.at[i], part_refs, known, col_ref, row_ref, e_ref[i], e_ref[2 + orb], amp)
            finish_pair(amp, amp_b, tilde.at[i], vv)

    return call(
        body,
        [jax.ShapeDtypeStruct((2, n, n), BF16), jax.ShapeDtypeStruct(vv.shape, F32)],
        [whole(pltpu.SMEM)] + [whole()] * (5 + len(parts)),
        [whole()] * 2,
        [pltpu.VMEM((n, n), F32), pltpu.VMEM((n, n), BF16)],
        flops=pair_flops(n, 0, 2) + 2 * 2 * n * (n - known) * nat.shape[2],
    )(energies, col, row, nat, *parts, amps, vv)


def gamma(tildes, orbitals, nat, first, count, before=None, left=None):
    n, naux = nat.shape[1:]
    depth = n * (2 + len(orbitals))
    counts = [len(parts) for parts in orbitals]
    start = left is None
    mine = [*tildes] if start else [left]

    def body(*refs):
        refs = list(refs)
        t_refs = [refs.pop(0) for _ in mine]
        nat_ref = refs.pop(0)
        part_refs = [[refs.pop(0) for _ in range(c)] for c in counts]
        if start:
            out, left_ref, right, buf, sems = refs
            for t, ref in enumerate(t_refs):
                left_ref[:, :, t * n : (t + 1) * n] = ref[...]
        else:
            _, out, right, buf, sems = refs
            left_ref = t_refs[0]
        copies = []
        for p in range(count):
            cols = slice((first + p) * TILE, (first + p + 1) * TILE)
            at = 0
            for j in range(2):
                right[:, at : at + n] = nat_ref[j, :, cols].T
                at += n
            for parts in part_refs:
                for ref in parts:
                    right[:, at : at + ref.shape[1]] = ref[cols, :]
                    at += ref.shape[1]
            for i in range(2):
                slot = 2 * p + i
                buf[slot] = lax.dot_general(left_ref[i], right[...], NT, preferred_element_type=F32)
                copies.append(pltpu.make_async_copy(buf.at[slot], out.at[i, :, cols], sems.at[slot]))
                copies[-1].start()
        for copy in copies:
            copy.wait()

    arrays = [*mine, nat] + [part for parts in orbitals for part in parts]
    specs = [whole()] * len(arrays)
    shapes, out_specs, aliases = [jax.ShapeDtypeStruct((2, n, naux), F32)], [whole(pltpu.HBM)], {}
    if start:
        shapes.append(jax.ShapeDtypeStruct((2, n, depth), BF16))
        out_specs.append(whole())
    else:
        arrays.append(before)
        specs.append(whole(pltpu.HBM))
        aliases = {len(arrays) - 1: 0}
    return call(
        body,
        shapes,
        specs,
        out_specs,
        [
            pltpu.VMEM((TILE, depth), BF16),
            pltpu.VMEM((2 * count, n, TILE), F32),
            pltpu.SemaphoreType.DMA((2 * count,)),
        ],
        aliases,
        flops=2 * 2 * n * depth * TILE * count,
        limit=10,
    )(*arrays)


def split_by_quarter(vv, quarter_id, quarters, blocks):
    n = vv.shape[0]
    rows = vv.reshape(blocks, quarters, n // (quarters * blocks), n)
    pick = lambda d: lax.dynamic_index_in_dim(rows, (quarter_id + d) % quarters, 1, keepdims=False)
    return [pick(0)] + [pick(d).astype(BF16) for d in range(1, quarters)]


def per_device(bints, occ_energy, vir_energy):
    quarters = lax.axis_size("quarter")
    blocks = lax.axis_size("blk")
    block_id = lax.axis_index("blk")
    quarter_id = lax.axis_index("quarter")
    odd = lax.rem(block_id, 2) == 1
    n = bints.shape[1]
    q = jnp.reshape(quarter_id, (1,)).astype(jnp.int32)

    def energies(step):
        group = (block_id + blocks - step) % blocks * quarters + quarter_id
        return lax.dynamic_slice_in_dim(occ_energy, group * 2, 2)

    def on_blk(x, by):
        return lax.ppermute(x, "blk", [(i, (i + by) % blocks) for i in range(blocks)])

    def swapped(x):
        return lax.ppermute(x, "blk", [(i, i ^ 1) for i in range(blocks)])

    def on_quarter(x, by):
        return lax.ppermute(x, "quarter", [(i, (i + by) % quarters) for i in range(quarters)])

    def on_both(x, by):
        return lax.ppermute(
            x,
            ("blk", "quarter"),
            [
                (b * quarters + k, (b + 2) % blocks * quarters + (k + by) % quarters)
                for b in range(blocks)
                for k in range(quarters)
            ],
        )

    def to_quarter(x, mask):
        return lax.ppermute(x, "quarter", [(i, i ^ mask) for i in range(quarters)])

    last = [bints]

    def gate(x):
        return lax.optimization_barrier((x, last[0]))[0]

    def done(x):
        last[0] = x
        return x

    def arrived(x):
        return done(gate(x))

    def relayed(from_two, mine):
        return swapped(done(jnp.where(odd, gate(from_two), mine)))

    def split(x):
        return [x[e] for e in range(quarters)]

    def join(pieces, widths):
        return done(joined([gate(pieces[0]), *pieces[1:]], q, widths))

    half, part = n // 2, n // 4
    raw, (g0, g1, g2) = slices(
        jnp.swapaxes(bints, 1, 2), q, (0, 0, half), ((0, half, half), (1, 0, n), (0, 0, half)), quarters
    )
    col, row = vir_energy[:, None], vir_energy[None, :]
    mine = energies(0)
    e0 = jnp.concatenate([mine, mine])
    e1 = jnp.concatenate([mine, energies(1)])
    e2 = jnp.concatenate([mine, energies(2)])

    raw2 = on_blk(raw, 2)
    r0 = [g0[0]] + [to_quarter(g0[e], e) for e in (1, 2, 3)]
    r1 = [g1[0]] + [to_quarter(g1[e], e) for e in (1, 2, 3)]
    r2 = [g2[0]] + [to_quarter(g2[e], e) for e in (1, 2, 3)]
    r0[1] = arrived(r0[1])
    r0[2] = arrived(r0[2])
    r0[3] = arrived(r0[3])
    (own23,) = join(r0, (half,))
    z0 = on_blk(own23, 2)
    raw2 = arrived(raw2)
    raw1 = relayed(raw2, raw)
    r1[3] = arrived(r1[3])
    r1[1] = arrived(r1[1])
    r1[2] = arrived(r1[2])
    own1 = join(r1, (half, part, part))
    z1, z2, z3 = (on_blk(x, 2) for x in own1)
    r2[2] = arrived(r2[2])
    r2[1] = arrived(r2[1])
    z0 = arrived(z0)
    x0 = relayed(z0, own23)
    r2[3] = arrived(r2[3])
    (own01,) = join(r2, (half,))
    raw1 = arrived(raw1)
    late = done(split(jnp.concatenate([raw2, gate(raw1)], axis=2)))
    rl = [late[0]] + [to_quarter(late[e], e) for e in (1, 2, 3)]
    nat, t00, t01, vv = done(own_pairs([gate([own01, own23]), own1], e0, col, row))
    z1 = arrived(z1)
    x1 = relayed(z1, own1[0])
    rl[1] = arrived(rl[1])
    z3 = arrived(z3)
    x3 = relayed(z3, own1[2])
    z2 = arrived(z2)
    x2 = relayed(z2, own1[1])
    x0 = arrived(x0)
    rl[2] = arrived(rl[2])
    two1 = [z1, z2, z3]
    t21, vv = done(other_pairs(nat, gate(two1), 1, e2, col, row, vv))
    rl[3] = arrived(rl[3])
    two01, one01 = join(rl, (half, half))
    x1 = arrived(x1)
    one0 = [one01, x0]
    t10, vv = done(other_pairs(nat, gate(one0), 0, e1, col, row, vv))
    x2 = arrived(x2)
    two0 = [two01, z0]
    t20, vv = done(other_pairs(nat, gate(two0), 0, e2, col, row, vv))
    amps = done(first_columns(nat, gate([x1, x2]), 1, e1, col, row))
    x3 = arrived(x3)
    one1 = [x1, x2, x3]
    t11, vv = done(last_columns(nat, gate([x3]), 1, e1, col, row, amps, vv))


    kept, *sent = split_by_quarter(vv, quarter_id, quarters, blocks)
    came = [on_quarter(s, d + 1) for d, s in enumerate(sent)]
    tildes, orbitals = [t00, t01, t20, t21, t10, t11], [two0, two1, one0, one1]
    density, left = done(gamma(tildes, orbitals, nat, 0, 2))
    total = kept + sum(gate(c).astype(F32) for c in came)
    tile, tiles = 2, nat.shape[2] // TILE

    part = n // (quarters * blocks)
    bit = 1
    while bit < blocks:
        mask = bit
        total = total.reshape(-1, 2, part, n)
        up = lax.rem(block_id // bit, 2)
        keep = lax.dynamic_index_in_dim(total, up, 1, keepdims=False)
        give = lax.dynamic_index_in_dim(total, 1 - up, 1, keepdims=False)
        got = lax.ppermute(give, "blk", [(i, i ^ mask) for i in range(blocks)])
        if tile < tiles:
            (density,) = done(gamma(tildes, orbitals, nat, tile, min(2, tiles - tile), density, left))
            tile += 2
        total = keep + gate(got)
        bit *= 2
    window = 2 * quarters * blocks * CYCLE * 2
    return density, total.reshape(part, n) / float(window)


def solution(mesh):
    return jax.shard_map(
        per_device,
        mesh=mesh,
        in_specs=(P("blk", None, "quarter"), P(), P()),
        out_specs=(P(("blk", "quarter"), None, None), P(("blk", "quarter"), None)),
        check_vma=False,
    )
```

```python
import jax
import jax.numpy as jnp
from jax import lax
from jax.experimental import pallas as pl
from jax.experimental.pallas import tpu as pltpu
from jax.sharding import PartitionSpec as P

CYCLE = 3
TILE = 256
F32, BF16 = jnp.float32, jnp.bfloat16
NT = (((1,), (1,)), ((), ()))


def whole(space=None):
    return pl.BlockSpec(memory_space=pltpu.VMEM if space is None else space)


def call(body, out_shape, in_specs, out_specs, scratch=(), aliases=None, flops=0, limit=8):
    return pl.pallas_call(
        body,
        out_shape=out_shape,
        in_specs=in_specs,
        out_specs=out_specs,
        scratch_shapes=list(scratch),
        input_output_aliases=aliases or {},
        compiler_params=pltpu.CompilerParams(vmem_limit_bytes=limit * 1024 * 1024),
        cost_estimate=pl.CostEstimate(flops=flops, bytes_accessed=0, transcendentals=0),
    )


def slices(bints, quarter_id, raw, groups, quarters):
    depth = bints.shape[1]

    def body(q_ref, src, *rest):
        outs, sems = rest[:-1], rest[-1]
        copies = []

        def copy(span, e, dst):
            orb, first, rows = span
            where = src.at[2 * (q_ref[0] ^ e) + orb, :, pl.ds(first, rows)]
            copies.append(pltpu.make_async_copy(where, dst, sems.at[len(copies)]))
            copies[-1].start()

        for r, span in enumerate(raw):
            for e in range(quarters):
                copy(span, e, outs[r].at[e])
        for g, span in enumerate(groups):
            for e in range(quarters):
                copy(span, e, outs[len(raw) + g * quarters + e])
        for c in copies:
            c.wait()

    shapes = [jax.ShapeDtypeStruct((quarters, depth, span[2]), BF16) for span in raw]
    shapes += [jax.ShapeDtypeStruct((depth, span[2]), BF16) for span in groups for _ in range(quarters)]
    flat = call(
        body,
        shapes,
        [whole(pltpu.SMEM), whole(pltpu.HBM)],
        [whole()] * len(shapes),
        [pltpu.SemaphoreType.DMA((quarters * (len(raw) + len(groups)),))],
    )(quarter_id, bints)
    rest = flat[len(raw) :]
    return flat[: len(raw)], [rest[g * quarters : (g + 1) * quarters] for g in range(len(groups))]


def joined(pieces, quarter_id, widths):
    depth = pieces[0].shape[0]

    def body(q_ref, *refs):
        ins, outs = refs[: len(pieces)], refs[len(pieces) :]
        for e, ref in enumerate(ins):
            rows = pl.ds(pl.multiple_of((q_ref[0] ^ e) * depth, 64), depth)
            at = 0
            for out, width in zip(outs, widths):
                out[rows, :] = ref[:, at : at + width]
                at += width

    return call(
        body,
        [jax.ShapeDtypeStruct((len(pieces) * depth, width), BF16) for width in widths],
        [whole(pltpu.SMEM)] + [whole()] * len(pieces),
        [whole()] * len(widths),
    )(quarter_id, *pieces)


def tiles_of(refs, first=0):
    found = []
    for ref in refs:
        for at in range(0, ref.shape[1], TILE):
            view = ref.at[:, at : min(at + TILE, ref.shape[1])]
            width = view.shape[1]
            if found and found[-1][1] + width <= TILE:
                found[-1] = (found[-1][0], found[-1][1] + width, found[-1][2] + [view])
            else:
                found.append((first, width, [view]))
            first += width
    return found


def side_by_side(values):
    return values[0] if len(values) == 1 else jnp.concatenate(values, axis=1)


def amplitudes(left, parts, first, col, row, e_left, e_right, amp):
    for at, width, views in tiles_of(parts, first):
        right = side_by_side([view[...] for view in views])
        pairint = jnp.dot(left[...], right, preferred_element_type=F32)
        cols = slice(at, at + width)
        amp[:, cols] = pairint / (col[...] + row[:, cols] - e_left - e_right)


def finish_pair(amp, amp_b, tilde, vv):
    size = amp.shape[0]
    for fa in range(0, size, TILE):
        for fb in range(0, size, TILE):
            here = amp[fa : fa + TILE, fb : fb + TILE]
            there = amp[fb : fb + TILE, fa : fa + TILE]
            amp_b[fa : fa + TILE, fb : fb + TILE] = here.astype(BF16)
            tilde[fa : fa + TILE, fb : fb + TILE] = (2.0 * here - there.T).astype(BF16)
    vv[...] += lax.dot_general(amp_b[...], tilde[...], NT, preferred_element_type=F32)


def pair_flops(n, naux, count):
    return count * 2 * n * n * (naux + n)


def own_pairs(own, energies, col, row):
    n = col.shape[0]
    naux = own[0][0].shape[0]
    counts = [len(parts) for parts in own]

    def body(e_ref, col_ref, row_ref, *refs):
        parts = [refs[: counts[0]], refs[counts[0] : sum(counts)]]
        nat, t0, t1, vv, amp, amp_b = refs[sum(counts) :]
        vv[...] = jnp.zeros_like(vv)
        for j in range(2):
            for first, width, views in tiles_of(parts[j]):
                nat[j, first : first + width, :] = side_by_side([view[...] for view in views]).T
        for j, tilde in enumerate((t0, t1)):
            for i in range(2):
                amplitudes(nat.at[i], parts[j], 0, col_ref, row_ref, e_ref[i], e_ref[2 + j], amp)
                finish_pair(amp, amp_b, tilde.at[i], vv)

    return call(
        body,
        [
            jax.ShapeDtypeStruct((2, n, naux), BF16),
            jax.ShapeDtypeStruct((2, n, n), BF16),
            jax.ShapeDtypeStruct((2, n, n), BF16),
            jax.ShapeDtypeStruct((n, n), F32),
        ],
        [whole(pltpu.SMEM)] + [whole()] * (2 + sum(counts)),
        [whole()] * 4,
        [pltpu.VMEM((n, n), F32), pltpu.VMEM((n, n), BF16)],
        flops=pair_flops(n, naux, 4),
    )(energies, col, row, *own[0], *own[1])


def other_pairs(nat, parts, orb, energies, col, row, vv):
    n = col.shape[0]

    def body(e_ref, col_ref, row_ref, nat_ref, *refs):
        part_refs = refs[: len(parts)]
        vv_in, tilde, vv, amp, amp_b = refs[len(parts) :]
        vv[...] = vv_in[...]
        for i in range(2):
            amplitudes(nat_ref.at[i], part_refs, 0, col_ref, row_ref, e_ref[i], e_ref[2 + orb], amp)
            finish_pair(amp, amp_b, tilde.at[i], vv)

    return call(
        body,
        [jax.ShapeDtypeStruct((2, n, n), BF16), jax.ShapeDtypeStruct(vv.shape, F32)],
        [whole(pltpu.SMEM)] + [whole()] * (4 + len(parts)),
        [whole()] * 2,
        [pltpu.VMEM((n, n), F32), pltpu.VMEM((n, n), BF16)],
        flops=pair_flops(n, nat.shape[2], 2),
    )(energies, col, row, nat, *parts, vv)


def first_columns(nat, parts, orb, energies, col, row):
    n = col.shape[0]
    wide = sum(part.shape[1] for part in parts)

    def body(e_ref, col_ref, row_ref, nat_ref, *refs):
        for i in range(2):
            amplitudes(nat_ref.at[i], refs[:-1], 0, col_ref, row_ref, e_ref[i], e_ref[2 + orb], refs[-1].at[i])

    return call(
        body,
        jax.ShapeDtypeStruct((2, n, wide), F32),
        [whole(pltpu.SMEM)] + [whole()] * (3 + len(parts)),
        whole(),
        flops=2 * 2 * n * wide * nat.shape[2],
    )(energies, col, row, nat, *parts)


def last_columns(nat, parts, orb, energies, col, row, amps, vv):
    n = col.shape[0]
    known = amps.shape[2]

    def body(e_ref, col_ref, row_ref, nat_ref, *refs):
        part_refs = refs[: len(parts)]
        amp_in, vv_in, tilde, vv, amp, amp_b = refs[len(parts) :]
        vv[...] = vv_in[...]
        for i in range(2):
            amp[:, :known] = amp_in[i]
            amplitudes(nat_ref.at[i], part_refs, known, col_ref, row_ref, e_ref[i], e_ref[2 + orb], amp)
            finish_pair(amp, amp_b, tilde.at[i], vv)

    return call(
        body,
        [jax.ShapeDtypeStruct((2, n, n), BF16), jax.ShapeDtypeStruct(vv.shape, F32)],
        [whole(pltpu.SMEM)] + [whole()] * (5 + len(parts)),
        [whole()] * 2,
        [pltpu.VMEM((n, n), F32), pltpu.VMEM((n, n), BF16)],
        flops=pair_flops(n, 0, 2) + 2 * 2 * n * (n - known) * nat.shape[2],
    )(energies, col, row, nat, *parts, amps, vv)


def gamma(tildes, orbitals, nat, first, count, before=None, left=None):
    n, naux = nat.shape[1:]
    depth = n * (2 + len(orbitals))
    counts = [len(parts) for parts in orbitals]
    start = left is None
    mine = [*tildes] if start else [left]

    def body(*refs):
        refs = list(refs)
        t_refs = [refs.pop(0) for _ in mine]
        nat_ref = refs.pop(0)
        part_refs = [[refs.pop(0) for _ in range(c)] for c in counts]
        if start:
            out, left_ref, right, buf, sems = refs
            for t, ref in enumerate(t_refs):
                left_ref[:, :, t * n : (t + 1) * n] = ref[...]
        else:
            _, out, right, buf, sems = refs
            left_ref = t_refs[0]
        copies = []
        for p in range(count):
            cols = slice((first + p) * TILE, (first + p + 1) * TILE)
            at = 0
            for j in range(2):
                right[:, at : at + n] = nat_ref[j, :, cols].T
                at += n
            for parts in part_refs:
                for ref in parts:
                    right[:, at : at + ref.shape[1]] = ref[cols, :]
                    at += ref.shape[1]
            for i in range(2):
                slot = 2 * p + i
                buf[slot] = lax.dot_general(left_ref[i], right[...], NT, preferred_element_type=F32)
                copies.append(pltpu.make_async_copy(buf.at[slot], out.at[i, :, cols], sems.at[slot]))
                copies[-1].start()
        for copy in copies:
            copy.wait()

    arrays = [*mine, nat] + [part for parts in orbitals for part in parts]
    specs = [whole()] * len(arrays)
    shapes, out_specs, aliases = [jax.ShapeDtypeStruct((2, n, naux), F32)], [whole(pltpu.HBM)], {}
    if start:
        shapes.append(jax.ShapeDtypeStruct((2, n, depth), BF16))
        out_specs.append(whole())
    else:
        arrays.append(before)
        specs.append(whole(pltpu.HBM))
        aliases = {len(arrays) - 1: 0}
    return call(
        body,
        shapes,
        specs,
        out_specs,
        [
            pltpu.VMEM((TILE, depth), BF16),
            pltpu.VMEM((2 * count, n, TILE), F32),
            pltpu.SemaphoreType.DMA((2 * count,)),
        ],
        aliases,
        flops=2 * 2 * n * depth * TILE * count,
        limit=10,
    )(*arrays)


def split_by_quarter(vv, quarter_id, quarters, blocks):
    n = vv.shape[0]
    rows = vv.reshape(blocks, quarters, n // (quarters * blocks), n)
    pick = lambda d: lax.dynamic_index_in_dim(rows, (quarter_id + d) % quarters, 1, keepdims=False)
    return [pick(0)] + [pick(d).astype(BF16) for d in range(1, quarters)]


def per_device(bints, occ_energy, vir_energy):
    quarters = lax.axis_size("quarter")
    blocks = lax.axis_size("blk")
    block_id = lax.axis_index("blk")
    quarter_id = lax.axis_index("quarter")
    odd = lax.rem(block_id, 2) == 1
    n = bints.shape[1]
    q = jnp.reshape(quarter_id, (1,)).astype(jnp.int32)

    def energies(step):
        group = (block_id + blocks - step) % blocks * quarters + quarter_id
        return lax.dynamic_slice_in_dim(occ_energy, group * 2, 2)

    def on_blk(x, by):
        return lax.ppermute(x, "blk", [(i, (i + by) % blocks) for i in range(blocks)])

    def swapped(x):
        return lax.ppermute(x, "blk", [(i, i ^ 1) for i in range(blocks)])

    def on_quarter(x, by):
        return lax.ppermute(x, "quarter", [(i, (i + by) % quarters) for i in range(quarters)])

    def on_both(x, by):
        return lax.ppermute(
            x,
            ("blk", "quarter"),
            [
                (b * quarters + k, (b + 2) % blocks * quarters + (k + by) % quarters)
                for b in range(blocks)
                for k in range(quarters)
            ],
        )

    def to_quarter(x, mask):
        return lax.ppermute(x, "quarter", [(i, i ^ mask) for i in range(quarters)])

    last = [bints]

    def gate(x):
        return lax.optimization_barrier((x, last[0]))[0]

    def done(x):
        last[0] = x
        return x

    def arrived(x):
        return done(gate(x))

    def relayed(from_two, mine):
        return swapped(done(jnp.where(odd, gate(from_two), mine)))

    def split(x):
        return [x[e] for e in range(quarters)]

    def join(pieces, widths):
        return done(joined([gate(pieces[0]), *pieces[1:]], q, widths))

    def exchanged(pieces):
        return [pieces[0]] + [to_quarter(pieces[e], e) for e in (1, 2, 3)]

    half, part = n // 2, n // 4
    (raw_a, raw_b), (g0, g1) = slices(
        jnp.swapaxes(bints, 1, 2), q, ((0, 0, half), (0, half, half)), ((1, 0, n), (0, 0, n)), quarters
    )
    col, row = vir_energy[:, None], vir_energy[None, :]
    mine = energies(0)
    e0 = jnp.concatenate([mine, mine])
    e1 = jnp.concatenate([mine, energies(1)])
    e2 = jnp.concatenate([mine, energies(2)])

    raw2a, raw2b = on_blk(raw_a, 2), on_blk(raw_b, 2)
    r0, r1 = exchanged(g0), exchanged(g1)
    r0[1] = arrived(r0[1])
    r1[1] = arrived(r1[1])
    r0[3] = arrived(r0[3])
    raw2b = arrived(raw2b)
    raw1b = relayed(raw2b, raw_b)
    r0[2] = arrived(r0[2])
    own1 = join(r0, (half, part, part))
    z0, z1, z2 = (on_blk(x, 2) for x in own1)
    r1[3] = arrived(r1[3])
    raw2a = arrived(raw2a)
    raw1a = relayed(raw2a, raw_a)
    r1[2] = arrived(r1[2])
    raw1b = arrived(raw1b)
    own0 = join(r1, (n,))
    z1 = arrived(z1)
    x1 = relayed(z1, own1[1])
    rl = exchanged(done(split(jnp.concatenate([raw2a, gate(raw2b)], axis=2))))
    nat, t00, t01, vv = done(own_pairs([gate(own0), own1], e0, col, row))
    rl[1] = arrived(rl[1])
    raw1a = arrived(raw1a)
    z0 = arrived(z0)
    rl[2] = arrived(rl[2])
    x0 = relayed(z0, own1[0])
    rm = exchanged(done(split(jnp.concatenate([raw1a, gate(raw1b)], axis=2))))
    x1 = arrived(x1)
    z2 = arrived(z2)
    two1 = [z0, z1, z2]
    t21, vv = done(other_pairs(nat, gate(two1), 1, e2, col, row, vv))
    rl[3] = arrived(rl[3])
    two0 = join(rl, (n,))
    x2 = relayed(z2, own1[2])
    rm[1] = arrived(rm[1])
    t20, vv = done(other_pairs(nat, gate(two0), 0, e2, col, row, vv))
    rm[2] = arrived(rm[2])
    x0 = arrived(x0)
    amps = done(first_columns(nat, gate([x0, x1]), 1, e1, col, row))
    rm[3] = arrived(rm[3])
    one0 = join(rm, (n,))
    t10, vv = done(other_pairs(nat, gate(one0), 0, e1, col, row, vv))
    x2 = arrived(x2)
    one1 = [x0, x1, x2]
    t11, vv = done(last_columns(nat, gate([x2]), 1, e1, col, row, amps, vv))

    kept, *sent = split_by_quarter(vv, quarter_id, quarters, blocks)
    came = [on_quarter(s, d + 1) for d, s in enumerate(sent)]
    tildes, orbitals = [t00, t01, t20, t21, t10, t11], [two0, two1, one0, one1]
    density, left = done(gamma(tildes, orbitals, nat, 0, 2))
    total = kept + sum(gate(c).astype(F32) for c in came)
    tile, tiles = 2, nat.shape[2] // TILE

    part = n // (quarters * blocks)
    bit = 1
    while bit < blocks:
        mask = bit
        total = total.reshape(-1, 2, part, n)
        up = lax.rem(block_id // bit, 2)
        keep = lax.dynamic_index_in_dim(total, up, 1, keepdims=False)
        give = lax.dynamic_index_in_dim(total, 1 - up, 1, keepdims=False)
        got = lax.ppermute(give, "blk", [(i, i ^ mask) for i in range(blocks)])
        if tile < tiles:
            (density,) = done(gamma(tildes, orbitals, nat, tile, min(2, tiles - tile), density, left))
            tile += 2
        total = keep + gate(got)
        bit *= 2
    window = 2 * quarters * blocks * CYCLE * 2
    return density, total.reshape(part, n) / float(window)


def solution(mesh):
    return jax.shard_map(
        per_device,
        mesh=mesh,
        in_specs=(P("blk", None, "quarter"), P(), P()),
        out_specs=(P(("blk", "quarter"), None, None), P(("blk", "quarter"), None)),
        check_vma=False,
    )
```
